128 devices in a mesh: inst: 16 (over z_lo, x, core), tp: 8 (over y, z_hi).
Axes of the slice: x: 4, y: 4, z: 4 (z_hi: 2, z_lo: 2; z = z_hi * 2 + z_lo), core: 2. Of those that a mesh axis runs over, the one named last changes fastest.
Arguments:
- inputs: bfloat16 [4, 2048, 5120], P(None, 'inst', 'tp'), may hold values from -6 to 6
- norm_gain: bfloat16 [5120], replicated, may hold values from 0.099609375 to 1.8984375
- query_weight: bfloat16 [5120, 4096], P(None, 'tp'), may hold values from -0.078125 to 0.078125
- key_weight: bfloat16 [5120, 1024], P(None, 'tp'), may hold values from -0.078125 to 0.078125
- value_weight: bfloat16 [5120, 1024], P(None, 'tp'), may hold values from -0.078125 to 0.078125
- output_weight: bfloat16 [4096, 5120], P('tp'), may hold values from -0.09375 to 0.09375
- query_gain: bfloat16 [128], replicated, may hold values from 0.5 to 2
- key_gain: bfloat16 [128], replicated, may hold values from 0.5 to 2
- kv_pool: bfloat16 [12288, 16, 2048], P('inst', None, 'tp'), may hold values from -68 to 68, as said below
- block_table: int32 [2048, 6], P('inst'), may hold values from 0 to 767, as said below
- cache_len: int32 [2048], P('inst'), may hold values from 1 to 96, 98304 in all
- move_block: int32 [4096], P('inst'), may hold values from 0 to 767
- move_target: int32 [4096, 1], P('inst'), may hold values from 0 to 15; in each aligned block of 256 rows (0 to 255, 256 to 511, ...) at most 64 rows name the same one
Outputs:
- mixed_out: bfloat16 [4, 2048, 5120], P(None, 'inst', 'tp')
- arrived: bfloat16 [16384, 16, 2048], P('inst', None, 'tp')
The draws below stay inside these ranges and needn't reach their ends.
Inputs may be any that keep to these rules, and one draw needn't show every extreme that they name: `block_table`: the rows of one instance name every block of its pool of 768 blocks exactly once. `cache_len`: some row holds exactly 96 tokens. `move_block`: a block of the source instance's pool; a block may be listed more than once. `move_target`: in the 256 moves of one instance no destination is named more than 64 times, and in some instance's list one destination is named exactly 64 times; a destination may be the source itself. `kv_pool`: cached keys and values.
All inputs are finite; a program needn't handle non-finite values. No bound on the sum of `cache_len` on one device may be relied on, other than what follows from the above.
Results may differ from the reference program's by a relative error of at most 0.017.
Values may be sent and summed in bfloat16 or wider, within the bound.
No kernel may reach another device: no remote copies, remote signals or barrier semaphores. Data moves between devices by JAX's collectives and lax.ppermute only.
A program may use at most 192 MiB of HBM per device.

```python
import math
import jax
import jax.numpy as jnp
import numpy as np
from jax import lax

D = 5120
KVH = 8
HEAD = 128
QH = 32
PAGE = 16
STEPS = 4
ROWS = 128
MAXB = 6
CAP = 64
INSTANCES = 16
POOL = 768
MOVES = 256
TOTAL_ROWS = 2048
TOTAL_BLOCKS = 12288
TOTAL_MOVES = 4096
N_INST = 16
N_TP = 8


def draw_kv_pool(key, part):
    key = jax.random.fold_in(key, 11)
    shape = (TOTAL_BLOCKS, PAGE, KVH * 2 * HEAD)
    return jnp.clip(jax.random.normal(key, shape, jnp.float32), -6.0, 6.0).astype(jnp.bfloat16)


def draw_block_table(key, part):
    key = jax.random.fold_in(key, 5)
    instance_count = TOTAL_ROWS // ROWS
    subkeys = jax.random.split(key, instance_count)
    orders = jax.vmap(lambda subkey: jax.random.permutation(subkey, POOL))(subkeys)
    return orders.reshape(TOTAL_ROWS, MAXB).astype(jnp.int32)


def set_ends(result, key, low, top_value):
    longest = result.shape.index(max(result.shape))
    spots = []
    for shift in (0, 1):
        where = [jax.random.randint(jax.random.fold_in(key, axis), (), 0, length) for axis, length in enumerate(result.shape)]
        where[longest] = (where[longest] + shift) % result.shape[longest]
        spots.append(tuple(where))
    return result.at[spots[0]].set(low).at[spots[1]].set(top_value)


def block_scale(key, dims, shards, low, high):
    factor_of, own = 1.0, jax.random.fold_in(key, 6)
    for axis_at, blocks in shards:
        heights = jnp.exp(jax.random.uniform(jax.random.fold_in(own, axis_at), (blocks,), jnp.float32, low / len(shards), high / len(shards)))
        factor_of = factor_of * jnp.repeat(heights, dims[axis_at] // blocks).reshape([-1 if axis == axis_at else 1 for axis in range(len(dims))])
    return factor_of


def profile(count, total, bound, slope):
    portions = [(1 << 20) // math.isqrt(grade ** slope) + 1 for grade in range(2, count + 1)]
    rest, holding = total - bound - (count - 1), [1] * (count - 1)
    while rest > 0:
        movable = [i for i in range(count - 1) if holding[i] < bound]
        pool, budget = sum([portions[i] for i in movable]), rest
        for i in movable:
            addition = min(bound - holding[i], max(1, budget * portions[i] // pool), rest)
            holding[i] = holding[i] + addition
            rest = rest - addition
    return np.array([bound] + holding)


def uneven_parts(key, amount, total, reach, skew):
    if amount == 2:
        one = jax.random.randint(key, (), max(1, total - reach), min(reach, total - 1) + 1)
        return jnp.stack([one, total - one])
    sizes = jnp.asarray(profile(amount, total, reach, skew), jnp.int32)
    twos = (amount - 1) // 2
    donor, taker = sizes[1:1 + 2 * twos:2], sizes[2:2 + 2 * twos:2]
    margin = jnp.minimum(donor - 1, reach - taker)
    shifted = jax.random.randint(jax.random.fold_in(key, 1), (twos,), 0, 1 << 20) % (margin + 1)
    sizes = sizes.at[1:1 + 2 * twos:2].set(donor - shifted).at[2:2 + 2 * twos:2].set(taker + shifted)
    return sizes[jax.random.permutation(jax.random.fold_in(key, 2), amount)]


def assign_block(stream_key, own, number, rows, amount, top, bound, skew):
    ranking = jax.random.permutation(stream_key, amount)
    heavy_load, usual = portions_of(amount, rows * top, bound, skew, True), portions_of(amount, rows * top, bound, skew, False)
    places = jnp.arange(amount)

    def named(sizes, offset_by):
        used = int((sizes > 0).sum())
        fixed = max(1, used // 4)
        moved = fixed + (places - fixed + offset_by * (used - fixed)) % max(1, amount - fixed)
        return jnp.zeros((amount,), jnp.int32).at[ranking[jnp.where(places < fixed, places, moved)]].set(jnp.asarray(sizes, jnp.int32))

    sizes = jnp.where(number % 4 == 0, named(heavy_load, number // 4), named(usual, number - number // 4 - 1))
    mixed = jax.random.permutation(jax.random.fold_in(own, 3), amount)
    giver, sink = mixed[0:amount // 2 * 2:2], mixed[1:amount // 2 * 2:2]
    room = jnp.minimum(sizes[giver] - 1, bound - sizes[sink]) // 2
    room = jnp.where((giver == ranking[0]) | (sink == ranking[0]) | (sizes[sink] == 0), 0, jnp.maximum(room, 0))
    moved = jax.random.randint(jax.random.fold_in(own, 4), (amount // 2,), 0, 1 << 20) % (room + 1)
    sizes = sizes.at[giver].add(-moved).at[sink].add(moved)
    items = jnp.searchsorted(jnp.cumsum(sizes), jnp.arange(rows * top), side="right").astype(jnp.int32)
    listing = items.reshape(top, rows).T
    listing = listing[jax.random.permutation(jax.random.fold_in(own, 1), rows)]
    offset_by = jax.random.randint(jax.random.fold_in(own, 2), (rows, 1), 0, top)
    return jnp.take_along_axis(listing, (jnp.arange(top)[None, :] + offset_by) % top, axis=1)


def portions_of(count, total, most, slope, full):
    weights = [(1 << 20) // math.isqrt(rank ** slope) + 1 for rank in range(1, count + 1)]
    largest = most if full else min(most, max(-(-total // count), total * weights[0] // sum(weights)))
    least = 1 if total - largest >= count - 1 else 0
    given, spare = [largest] + [least] * (count - 1), total - largest - least * (count - 1)
    while spare > 0:
        candidates = [i for i in range(1, count) if given[i] < largest] or [i for i in range(1, count) if given[i] < most]
        mass, left = sum([weights[i] for i in candidates]), spare
        for i in candidates:
            addition = min(most - given[i], max(1, left * weights[i] // mass), spare)
            given[i] = given[i] + addition
            spare = spare - addition
    return np.array(given)


def noise(own_key, extent, scale, reach, shards=(), held_as=jnp.bfloat16):
    array = scale * jax.random.normal(own_key, extent, jnp.float32)
    if shards:
        array = array * block_scale(own_key, extent, shards, -0.22, 0.18)
    return jnp.clip(array, -reach, reach).astype(held_as)


def setup_inputs(seed: int = 0) -> dict:
    streams_of = jax.random.split(jax.random.key(seed), 14)
    inputs = noise(streams_of[0], (STEPS, TOTAL_ROWS, D), 1.0, 6.0, ((1, 16), (2, 8)))
    norm_gain = jnp.clip(1.0 + 0.18 * jax.random.normal(streams_of[1], (D,), jnp.float32), 0.099609375, 1.8984375).astype(jnp.bfloat16)
    query_weight = noise(streams_of[2], (D, QH * HEAD), D ** -0.5, 0.078125, ((1, 8),))
    key_weight = noise(streams_of[3], (D, KVH * HEAD), D ** -0.5, 0.078125, ((1, 8),))
    value_weight = noise(streams_of[4], (D, KVH * HEAD), D ** -0.5, 0.078125, ((1, 8),))
    output_weight = noise(streams_of[5], (QH * HEAD, D), (QH * HEAD) ** -0.5, 0.09375, ((0, 8),))
    query_gain = jnp.clip(jnp.exp(jax.random.uniform(streams_of[6], (HEAD,), jnp.float32, math.log(0.5), math.log(2.0))), 0.5, 2.0).astype(jnp.bfloat16)
    key_gain = jnp.clip(jnp.exp(jax.random.uniform(streams_of[7], (HEAD,), jnp.float32, math.log(0.5), math.log(2.0))), 0.5, 2.0).astype(jnp.bfloat16)
    kv_pool = draw_kv_pool(jax.random.fold_in(streams_of[13], 71), 0)
    block_table = draw_block_table(jax.random.fold_in(streams_of[13], 71), 0)
    cache_len = uneven_parts(streams_of[10], TOTAL_ROWS, TOTAL_ROWS * MAXB * PAGE // 2, MAXB * PAGE, 2).astype(jnp.int32)
    move_block = set_ends(jax.random.randint(streams_of[11], (TOTAL_MOVES,), 0, POOL), jax.random.fold_in(streams_of[11], 1), 0, POOL - 1).astype(jnp.int32)
    move_target_keys = jax.random.split(jax.random.fold_in(streams_of[12], 1), TOTAL_MOVES // MOVES)
    move_target_turns = jax.random.permutation(jax.random.fold_in(streams_of[12], 3), TOTAL_MOVES // MOVES)
    move_target = jax.vmap(lambda own, number: assign_block(jax.random.fold_in(streams_of[12], 2), own, number, MOVES, INSTANCES, 1, CAP, 2))(move_target_keys, move_target_turns).reshape((TOTAL_MOVES, 1))
    return {"inputs": inputs, "norm_gain": norm_gain, "query_weight": query_weight, "key_weight": key_weight, "value_weight": value_weight, "output_weight": output_weight, "query_gain": query_gain, "key_gain": key_gain, "kv_pool": kv_pool, "block_table": block_table, "cache_len": cache_len, "move_block": move_block, "move_target": move_target}


EPSILON = 1e-06

def rms_rows(values, gain_f32):
    mean_square = lax.optimization_barrier(jnp.mean(values * values, axis=-1, keepdims=True))
    return values * lax.rsqrt(mean_square + EPSILON) * gain_f32

def attend_cache(queries, cache_keys, cache_values, new_keys, new_values, lengths):
    highest = lax.Precision.HIGHEST
    step_count = queries.shape[0]
    places = cache_keys.shape[1]
    score_scale = HEAD ** (-0.5)
    cache_scores = jnp.einsum('srkgh,rpkh->srkgp', queries.astype(jnp.float32), cache_keys.astype(jnp.float32), precision=highest) * score_scale
    fresh_scores = jnp.einsum('srkgh,urkh->srkgu', queries.astype(jnp.float32), new_keys.astype(jnp.float32), precision=highest) * score_scale
    cache_ok = (jnp.arange(places)[None, :] < lengths[:, None])[None, :, None, None, :]
    fresh_ok = (jnp.arange(step_count)[None, :] <= jnp.arange(step_count)[:, None])[:, None, None, None, :]
    cache_scores = jnp.where(cache_ok, cache_scores, -jnp.inf)
    fresh_scores = jnp.where(fresh_ok, fresh_scores, -jnp.inf)
    highest_score = jnp.maximum(lax.optimization_barrier(jnp.max(cache_scores, axis=-1, keepdims=True)), lax.optimization_barrier(jnp.max(fresh_scores, axis=-1, keepdims=True)))
    cache_exp = jnp.exp(cache_scores - highest_score)
    fresh_exp = jnp.exp(fresh_scores - highest_score)
    denominator = lax.optimization_barrier(jnp.sum(cache_exp, axis=-1, keepdims=True)) + lax.optimization_barrier(jnp.sum(fresh_exp, axis=-1, keepdims=True))
    cache_weights = (cache_exp / denominator).astype(jnp.bfloat16)
    fresh_weights = (fresh_exp / denominator).astype(jnp.bfloat16)
    context = jnp.einsum('srkgp,rpkh->srkgh', cache_weights.astype(jnp.float32), cache_values.astype(jnp.float32), precision=highest)
    context = context + jnp.einsum('srkgu,urkh->srkgh', fresh_weights.astype(jnp.float32), new_values.astype(jnp.float32), precision=highest)
    return context.astype(jnp.bfloat16)

def decode_one(x_rows, table, lengths, pool_rows, norm_gain, query_weight, key_weight, value_weight, output_weight, query_gain, key_gain):
    step_count, row_count, width = x_rows.shape
    flattened = x_rows.reshape(step_count * row_count, width).astype(jnp.float32)
    normed = rms_rows(flattened, norm_gain.astype(jnp.float32)).astype(jnp.bfloat16)
    queries = jnp.dot(normed, query_weight, preferred_element_type=jnp.float32).reshape(step_count, row_count, KVH, QH // KVH, HEAD)
    queries = rms_rows(queries, query_gain.astype(jnp.float32)).astype(jnp.bfloat16)
    new_keys = jnp.dot(normed, key_weight, preferred_element_type=jnp.float32).reshape(step_count, row_count, KVH, HEAD)
    new_keys = rms_rows(new_keys, key_gain.astype(jnp.float32)).astype(jnp.bfloat16)
    new_values = jnp.dot(normed, value_weight, preferred_element_type=jnp.float32).astype(jnp.bfloat16).reshape(step_count, row_count, KVH, HEAD)
    cached = pool_rows[table].reshape(row_count, MAXB * PAGE, KVH, 2, HEAD)
    context = attend_cache(queries, cached[:, :, :, 0], cached[:, :, :, 1], new_keys, new_values, lengths)
    context = context.reshape(step_count * row_count, QH * HEAD)
    part_width = QH * HEAD // N_TP
    summed = jnp.zeros((step_count * row_count, width), jnp.float32)
    for group_index in range(N_TP):
        lower = group_index * part_width
        partial_value = jnp.dot(context[:, lower:lower + part_width], output_weight[lower:lower + part_width], preferred_element_type=jnp.float32)
        rounded = lax.optimization_barrier(partial_value.astype(jnp.bfloat16))
        summed = summed + rounded.astype(jnp.float32)
    return summed.astype(jnp.bfloat16).reshape(step_count, row_count, width)

def send_rows(target, blocks, pool_count):
    onehot = (target[:, None] == jnp.arange(N_INST, dtype=jnp.int32)[None, :]).astype(jnp.int32)
    order_in = lax.optimization_barrier(jnp.sum((jnp.cumsum(onehot, axis=0) - onehot) * onehot, axis=1)).astype(jnp.int32)
    slots = (target * CAP + order_in).astype(jnp.int32)
    return jnp.full((N_INST * CAP,), pool_count, jnp.int32).at[slots].set(blocks.astype(jnp.int32))

def reference(inputs, norm_gain, query_weight, key_weight, value_weight, output_weight, query_gain, key_gain, kv_pool, block_table, cache_len, move_block, move_target):
    step_count = inputs.shape[0]
    width = inputs.shape[2]
    lanes = kv_pool.shape[2]
    x_all = inputs.reshape(step_count, N_INST, ROWS, width).transpose(1, 0, 2, 3)
    tables = block_table.reshape(N_INST, ROWS, MAXB)
    lengths = cache_len.reshape(N_INST, ROWS)
    pools = kv_pool.reshape(N_INST, POOL, PAGE, lanes)

    def run_instance(pieces):
        x_rows, table, length_rows, pool_rows = pieces
        return decode_one(x_rows, table, length_rows, pool_rows, norm_gain, query_weight, key_weight, value_weight, output_weight, query_gain, key_gain)
    mixed_all = lax.map(run_instance, (x_all, tables, lengths, pools))
    mixed_out = mixed_all.transpose(1, 0, 2, 3).reshape(step_count, N_INST * ROWS, width)
    blocks = move_block.reshape(N_INST, MOVES)
    targets = move_target[:, 0].reshape(N_INST, MOVES)

    def send_instance(pieces):
        pool_rows, block_rows, target_rows = pieces
        source_rows = send_rows(target_rows, block_rows, POOL)
        return jnp.take(pool_rows, source_rows, axis=0, mode='fill', fill_value=0)
    outgoing = lax.map(send_instance, (pools, blocks, targets))
    arrived = outgoing.reshape(N_INST, N_INST, CAP, PAGE, lanes).transpose(1, 0, 2, 3, 4).reshape(N_INST * N_INST * CAP, PAGE, lanes)
    return (mixed_out, arrived)
```

```python
import functools

import jax
import jax.numpy as jnp
from jax import lax
from jax.experimental import pallas as pl
from jax.experimental.pallas import tpu as pltpu
from jax.sharding import PartitionSpec as P

HEAD = 128
CAP = 64
PAGE = 16
EPSILON = 1e-06
GROUP = 8
CHUNKS = 2
NEG = -1e30
MIB = 1024 * 1024

GATHERED = ((0, 0), (0, 1), (1, 0), (3, 0), (2, 0), (1, 1), (3, 1), (2, 1))
SCATTERED = ((2, 0), (1, 1), (2, 1), (3, 0), (1, 0), (3, 1), (0, 0), (0, 1))


def places(relative):
    me = lax.axis_index("tp")
    y, z = me // 2, me % 2
    return jnp.stack([((y + dy) % 4) * 2 + (z + dz) % 2 for dy, dz in relative]).astype(jnp.int32)


def tp_move(array, dy, dz):
    pairs = [(y * 2 + z, ((y + dy) % 4) * 2 + (z + dz) % 2) for y in range(4) for z in range(2)]
    return lax.ppermute(array, "tp", pairs)


def inst_move(array, dz, dx, dc):
    pairs = [
        (z * 8 + x * 2 + c, ((z + dz) % 2) * 8 + ((x + dx) % 4) * 2 + (c + dc) % 2)
        for z in range(2)
        for x in range(4)
        for c in range(2)
    ]
    return lax.ppermute(array, "inst", pairs)


def decode_kernel(
    rows, first_row, sources, targets, table, x0, x1, x2, x3, x4, x5, x6, x7, gain, wq, wk, wv, wo, pool,
    lane_row, query_gain, key_gain, plus, minus, local,
    x_v, wq_v, wk_v, wv_v, wo_v, pool_v, qkv, ctx, out_v, sems,
):
    steps = 4
    groups = 4
    width = x0.shape[2]
    count = steps * rows
    xs = (x0, x1, x2, x3, x4, x5, x6, x7)
    w_copies, o_copies = [], []
    for k in range(8):
        span = pl.ds(pl.multiple_of(sources[k] * width, width), width)
        w_copies.append(
            (
                pltpu.make_async_copy(wq.at[span], wq_v.at[k], sems.at[0, k]),
                pltpu.make_async_copy(wk.at[span], wk_v.at[k], sems.at[1, k]),
                pltpu.make_async_copy(wv.at[span], wv_v.at[k], sems.at[2, k]),
            )
        )
        span = pl.ds(pl.multiple_of(targets[k] * width, 128), width)
        o_copies.append(pltpu.make_async_copy(wo.at[:, span], wo_v.at[k], sems.at[3, k]))
    pool_copy = pltpu.make_async_copy(pool, pool_v, sems.at[4, 0])
    x_copies = [
        pltpu.make_async_copy(xs[k].at[:, pl.ds(first_row, rows)], x_v.at[k], sems.at[5, k])
        for k in range(8)
    ]
    for copy in x_copies:
        copy.start()
    for trio in w_copies:
        for copy in trio:
            copy.start()
    pool_copy.start()
    for copy in o_copies:
        copy.start()

    square = jnp.zeros((count, 1), jnp.float32)
    for k in range(8):
        x_copies[k].wait()
        part = x_v[k].reshape(count, width).astype(jnp.float32)
        square = square + jnp.sum(part * part, axis=1, keepdims=True)
    inverse = lax.rsqrt(square * (1.0 / (8 * width)) + EPSILON)
    for k in range(8):
        for copy in w_copies[k]:
            copy.wait()
        normed = x_v[k].reshape(count, width).astype(jnp.float32) * inverse * gain[sources[k]]
        normed = normed.astype(jnp.bfloat16)
        q_part = jnp.dot(normed, wq_v[k], preferred_element_type=jnp.float32)
        k_part = jnp.dot(normed, wk_v[k], preferred_element_type=jnp.float32)
        v_part = jnp.dot(normed, wv_v[k], preferred_element_type=jnp.float32)
        if k == 0:
            qkv[:, 0:512] = q_part
            qkv[:, 512:640] = k_part
            qkv[:, 640:768] = v_part
        else:
            qkv[:, 0:512] += q_part
            qkv[:, 512:640] += k_part
            qkv[:, 640:768] += v_part
    for head in range(5):
        lanes = slice(head * HEAD, (head + 1) * HEAD)
        raw = qkv[:, lanes]
        mean = jnp.mean(raw * raw, axis=1, keepdims=True)
        head_gain = query_gain[...] if head < 4 else key_gain[...]
        qkv[:, lanes] = raw * lax.rsqrt(mean + EPSILON) * head_gain

    pool_copy.wait()
    height = steps * groups * GROUP
    query_row = lax.broadcasted_iota(jnp.int32, (height, 1), 0) % GROUP
    query_step = lax.broadcasted_iota(jnp.int32, (height, 1), 0) // (groups * GROUP)
    fresh_lane = lax.broadcasted_iota(jnp.int32, (1, steps * GROUP), 1)
    fresh_ok = (fresh_lane % GROUP == query_row) & (fresh_lane // GROUP <= query_step)
    scale = HEAD ** (-0.5)
    contract_last = (((1,), (1,)), ((), ()))

    def attend(i, carry):
        first = pl.multiple_of(i * GROUP, GROUP)

        def tiles(lane):
            return [
                qkv[pl.ds(pl.multiple_of(t * rows + first, GROUP), GROUP), lane * HEAD : (lane + 1) * HEAD]
                for t in range(steps)
            ]

        per_group = [tiles(g) for g in range(groups)]
        queries = jnp.concatenate(
            [per_group[g][t] for t in range(steps) for g in range(groups)], axis=0
        ).astype(jnp.bfloat16)
        fresh_k = jnp.concatenate(tiles(4), axis=0).astype(jnp.bfloat16)
        fresh_v = jnp.concatenate(tiles(5), axis=0).astype(jnp.bfloat16)
        blocks = [pool_v[table[i * (GROUP * 6) + j]] for j in range(GROUP * 6)]
        cached_k = jnp.concatenate([b[:, :HEAD] for b in blocks], axis=0)
        cached_v = jnp.concatenate([b[:, HEAD:] for b in blocks], axis=0)
        scores = lax.dot_general(queries, cached_k, contract_last, preferred_element_type=jnp.float32)
        fresh = lax.dot_general(queries, fresh_k, contract_last, preferred_element_type=jnp.float32)
        scores = jnp.where(lane_row[i] == query_row, scores * scale, NEG)
        fresh = jnp.where(fresh_ok, fresh * scale, NEG)
        top = jnp.maximum(
            jnp.max(scores, axis=1, keepdims=True), jnp.max(fresh, axis=1, keepdims=True)
        )
        weights = jnp.exp(scores - top)
        fresh_weights = jnp.exp(fresh - top)
        total = jnp.sum(weights, axis=1, keepdims=True) + jnp.sum(
            fresh_weights, axis=1, keepdims=True
        )
        mixed = jnp.dot(weights.astype(jnp.bfloat16), cached_v, preferred_element_type=jnp.float32)
        mixed += jnp.dot(
            fresh_weights.astype(jnp.bfloat16), fresh_v, preferred_element_type=jnp.float32
        )
        mixed = mixed / total
        for t in range(steps):
            for g in range(groups):
                at = (t * groups + g) * GROUP
                ctx[
                    pl.ds(pl.multiple_of(t * rows + first, GROUP), GROUP),
                    g * HEAD : (g + 1) * HEAD,
                ] = mixed[at : at + GROUP]
        return carry

    lax.fori_loop(0, rows // GROUP, attend, 0, unroll=2)

    context = ctx[...].astype(jnp.bfloat16)
    outs = [plus.at[0], plus.at[1], minus.at[0], minus.at[1]] + [local.at[j] for j in range(4)]
    out_copies = []
    for k in range(8):
        o_copies[k].wait()
        out_v[k] = jnp.dot(context, wo_v[k], preferred_element_type=jnp.float32).astype(jnp.bfloat16)
        out_copies.append(pltpu.make_async_copy(out_v.at[k], outs[k], sems.at[6, k]))
        out_copies[k].start()
    for copy in out_copies:
        copy.wait()


def decode(
    rows, first_row, sources, targets, table, xs, gain, wq, wk, wv, wo, pool, lane_row, query_gain, key_gain
):
    steps, _, width = xs[0].shape
    count = steps * rows
    bf16, f32 = jnp.bfloat16, jnp.float32
    smem = pl.BlockSpec(memory_space=pltpu.SMEM)
    vmem = pl.BlockSpec(memory_space=pltpu.VMEM)
    hbm = pl.BlockSpec(memory_space=pltpu.HBM)
    return pl.pallas_call(
        functools.partial(decode_kernel, rows, first_row),
        out_shape=(
            jax.ShapeDtypeStruct((2, count, width), bf16),
            jax.ShapeDtypeStruct((2, count, width), bf16),
            jax.ShapeDtypeStruct((4, count, width), bf16),
        ),
        in_specs=[smem] * 3 + [hbm] * 8 + [vmem] + [hbm] * 5 + [vmem] * 3,
        out_specs=(hbm, hbm, hbm),
        scratch_shapes=[
            pltpu.VMEM((8, steps, rows, width), bf16),
            pltpu.VMEM((8, width, wq.shape[1]), bf16),
            pltpu.VMEM((8, width, wk.shape[1]), bf16),
            pltpu.VMEM((8, width, wv.shape[1]), bf16),
            pltpu.VMEM((8, wo.shape[0], width), bf16),
            pltpu.VMEM(pool.shape, bf16),
            pltpu.VMEM((count, 768), f32),
            pltpu.VMEM((count, 512), f32),
            pltpu.VMEM((8, count, width), bf16),
            pltpu.SemaphoreType.DMA((7, 8)),
        ],
        compiler_params=pltpu.CompilerParams(vmem_limit_bytes=60 * MIB),
        cost_estimate=pl.CostEstimate(
            flops=2 * count * 5120 * 1280, bytes_accessed=24 * MIB, transcendentals=0
        ),
        name="decode_rows",
    )(sources, targets, table, *xs, gain, wq, wk, wv, wo, pool, lane_row, query_gain, key_gain)


def slots_kernel(table, order, blocks, *refs):
    outs, (blocks_v, sems) = refs[:-7], refs[-2:]
    stages = refs[-7:-2]
    load = pltpu.make_async_copy(blocks, blocks_v, sems.at[0])
    load.start()
    load.wait()
    copies = []
    if len(outs) == 5:

        def pick(m, carry):
            stages[4][m] = blocks_v[order[m]]
            return carry

        lax.fori_loop(0, outs[4].shape[0], pick, 0, unroll=8)
        copies.append(pltpu.make_async_copy(stages[4], outs[4], sems.at[5]))
        copies[0].start()
    for d in (2, 1, 3, 0):

        def one(j, carry):
            at = table[d * 2 * CAP + j]
            block = blocks_v[jnp.maximum(at, 0)]
            stages[d][j] = jnp.where(at >= 0, block, jnp.zeros_like(block))
            return carry

        lax.fori_loop(0, 2 * CAP, one, 0, unroll=8)
        copies.append(pltpu.make_async_copy(stages[d], outs[d], sems.at[1 + d]))
        copies[-1].start()
    for copy in copies:
        copy.wait()


def fill_slots(table, order, blocks, with_compact):
    smem = pl.BlockSpec(memory_space=pltpu.SMEM)
    hbm = pl.BlockSpec(memory_space=pltpu.HBM)
    tail = blocks.shape[1:]
    heights = [2 * CAP] * 4 + [order.shape[0]] * with_compact
    return pl.pallas_call(
        slots_kernel,
        out_shape=tuple(jax.ShapeDtypeStruct((n,) + tail, blocks.dtype) for n in heights),
        in_specs=[smem, smem, hbm],
        out_specs=(hbm,) * len(heights),
        scratch_shapes=[pltpu.VMEM((2 * CAP,) + tail, blocks.dtype)] * 4
        + [
            pltpu.VMEM((order.shape[0],) + tail, blocks.dtype),
            pltpu.VMEM(blocks.shape, blocks.dtype),
            pltpu.SemaphoreType.DMA((6,)),
        ],
        compiler_params=pltpu.CompilerParams(vmem_limit_bytes=60 * MIB),
        cost_estimate=pl.CostEstimate(flops=0, bytes_accessed=16 * MIB, transcendentals=0),
        name="fill_slots",
    )(table, order, blocks)


def slot_table(target, values, own_z, own_x, own_c):
    order = jnp.arange(target.shape[0], dtype=jnp.int32)
    earlier = (target[:, None] == target[None, :]) & (order[None, :] < order[:, None])
    rank = jnp.sum(earlier.astype(jnp.int32), axis=1)
    slot = jnp.arange(8 * CAP, dtype=jnp.int32)
    far, other = slot // (2 * CAP), (slot // CAP) % 2
    wanted = own_z * 8 + ((own_x + far) % 4) * 2 + (own_c + other) % 2
    match = (wanted * CAP + slot % CAP)[:, None] == (target * CAP + rank)[None, :]
    return jnp.max(jnp.where(match, values[None, :], -1), axis=1)


def cross(received):
    return received + [inst_move(r, 0, 0, 1) for r in received]


def place_kernel(places_ref, *refs):
    pieces, out, stage, sems = refs[:8], refs[-3], refs[-2], refs[-1]
    ins, outs = [], []
    for j in range(8):
        start = pl.multiple_of(places_ref[j] * CAP, CAP)
        part = pieces[j].at[pl.ds((j // 4) * CAP, CAP)]
        ins.append(pltpu.make_async_copy(part, stage.at[j], sems.at[0, j]))
        outs.append(pltpu.make_async_copy(stage.at[j], out.at[pl.ds(start, CAP)], sems.at[1, j]))
    for copy in ins:
        copy.start()
    for j in range(8):
        ins[j].wait()
        outs[j].start()
    for copy in outs:
        copy.wait()


def place_pieces(where, pieces, before):
    smem = pl.BlockSpec(memory_space=pltpu.SMEM)
    either = pl.BlockSpec(memory_space=pl.ANY)
    hbm = pl.BlockSpec(memory_space=pltpu.HBM)
    blocks = pieces[0].shape[1:]
    shape = jax.ShapeDtypeStruct((16 * CAP,) + blocks, pieces[0].dtype)
    extra = [] if before is None else [before]
    return pl.pallas_call(
        place_kernel,
        out_shape=shape,
        in_specs=[smem] + [either] * 8 + [hbm] * len(extra),
        out_specs=hbm,
        scratch_shapes=[
            pltpu.VMEM((8, CAP) + blocks, pieces[0].dtype),
            pltpu.SemaphoreType.DMA((2, 8)),
        ],
        input_output_aliases={} if before is None else {9: 0},
        compiler_params=pltpu.CompilerParams(vmem_limit_bytes=60 * MIB),
        cost_estimate=pl.CostEstimate(flops=0, bytes_accessed=16 * MIB, transcendentals=0),
        name="place_pieces",
    )(where, *pieces, *extra)


def after(array, *others):
    return lax.optimization_barrier((array,) + others)[0]


def gather_rows(x):
    other = tp_move(x, 0, 1)
    up, down = tp_move(x, 3, 0), tp_move(x, 1, 0)
    other_up, other_down = tp_move(other, 3, 0), tp_move(other, 1, 0)
    far = tp_move(down, 1, 0)
    other_far = tp_move(other_up, 3, 0)
    return [x, other, up, down, far, other_up, other_down, other_far]


def scatter_sum(plus, minus, local):
    f32, bf16 = jnp.float32, jnp.bfloat16
    below = tp_move(plus, 1, 0)
    above = tp_move(minus, 3, 0)
    up = (local[0].astype(f32) + below[0].astype(f32)).astype(bf16)
    down = (local[1].astype(f32) + above[0].astype(f32)).astype(bf16)
    from_below = tp_move(up, 1, 0)
    from_above = tp_move(down, 3, 0)
    other = (local[3].astype(f32) + below[1].astype(f32) + from_above.astype(f32)).astype(bf16)
    crossed = tp_move(other, 0, 1)
    mine = local[2].astype(f32) + above[1].astype(f32) + from_below.astype(f32)
    return (mine + crossed.astype(f32)).astype(bf16)


def body(
    inputs,
    norm_gain,
    query_weight,
    key_weight,
    value_weight,
    output_weight,
    query_gain,
    key_gain,
    kv_pool,
    block_table,
    cache_len,
    move_block,
    move_target,
):
    step_count, row_count, width = inputs.shape
    f32 = jnp.float32
    own = lax.axis_index("inst")
    own_z, own_x, own_c = own // 8, (own // 2) % 4, own % 2

    target = move_target[:, 0]
    other_target = inst_move(target, 1, 0, 0)

    rows = row_count // CHUNKS
    gathered = gather_rows(inputs)

    table = slot_table(target, move_block, own_z, own_x, own_c)
    table = after(table, gathered[1])
    *slots, compact = fill_slots(table, move_block, kv_pool, True)
    compact = after(compact, other_target)
    other_target = after(other_target, compact)
    other_blocks = inst_move(compact, 1, 0, 0)
    far = inst_move(slots[2], 0, 2, 0)
    near = inst_move(after(slots[1], far, gathered[5]), 0, 1, 0)
    back = inst_move(after(slots[3], far, gathered[5]), 0, 3, 0)
    order = jnp.arange(move_block.shape[0], dtype=jnp.int32)
    other_table = slot_table(other_target, order, own_z, own_x, own_c)

    gain = norm_gain.astype(f32).reshape(8, 1, width)
    positions = jnp.arange(block_table.shape[1] * PAGE, dtype=jnp.int32)
    lane_row = jnp.where(
        positions[None, :] < cache_len[:, None],
        (jnp.arange(row_count, dtype=jnp.int32) % GROUP)[:, None],
        -1,
    ).reshape(row_count // GROUP, 1, -1)
    sources, targets = places(GATHERED), places(SCATTERED)
    query_gain = query_gain.astype(f32).reshape(1, HEAD)
    key_gain = key_gain.astype(f32).reshape(1, HEAD)
    def where(z):
        return jnp.stack(
            [z * 8 + ((own_x - j % 4) % 4) * 2 + (own_c + j // 4) % 2 for j in range(8)]
        ).astype(jnp.int32)

    arrived = place_pieces(where(own_z), cross([slots[0], near, far, back]), None)

    chunks = []
    for c in range(CHUNKS):
        first = c * rows
        tables = block_table[first : first + rows].reshape(-1)
        lanes = lane_row[first // GROUP : (first + rows) // GROUP]
        if c == 1:
            other_table = after(other_table, parts[0])
            other_slots = fill_slots(other_table, order, other_blocks, False)
            other_near = inst_move(other_slots[1], 0, 1, 0)
            other_back = inst_move(other_slots[3], 0, 3, 0)
            gathered[0] = after(gathered[0], other_slots[0])
        parts = decode(
            rows, first, sources, targets, tables, gathered, gain, query_weight, key_weight,
            value_weight, output_weight, kv_pool, lanes, query_gain, key_gain,
        )
        chunks.append(scatter_sum(*parts).reshape(step_count, rows, width))
    mixed_out = jnp.concatenate(chunks, axis=1)

    other_far = inst_move(after(other_slots[2], arrived, other_near, other_back), 0, 2, 0)
    other_pieces = cross([other_slots[0], other_near, other_far, other_back])
    arrived = place_pieces(where(1 - own_z), other_pieces, arrived)
    return (mixed_out, arrived)


def solution(mesh):
    in_specs = (
        P(None, "inst", "tp"),
        P(),
        P(None, "tp"),
        P(None, "tp"),
        P(None, "tp"),
        P("tp", None),
        P(),
        P(),
        P("inst", None, "tp"),
        P("inst", None),
        P("inst"),
        P("inst"),
        P("inst", None),
    )
    out_specs = (P(None, "inst", "tp"), P("inst", None, "tp"))
    return jax.shard_map(body, mesh=mesh, in_specs=in_specs, out_specs=out_specs, check_vma=False)
```

```python
import functools

import jax
import jax.numpy as jnp
from jax import lax
from jax.experimental import pallas as pl
from jax.experimental.pallas import tpu as pltpu
from jax.sharding import PartitionSpec as P

HEAD = 128
CAP = 64
PAGE = 16
EPSILON = 1e-06
GROUP = 8
CHUNKS = 2
NEG = -1e30
MIB = 1024 * 1024

GATHERED = ((0, 0), (0, 1), (1, 0), (3, 0), (2, 0), (1, 1), (3, 1), (2, 1))
SCATTERED = ((2, 0), (1, 1), (2, 1), (3, 0), (1, 0), (3, 1), (0, 0), (0, 1))


def places(relative):
    me = lax.axis_index("tp")
    y, z = me // 2, me % 2
    return jnp.stack([((y + dy) % 4) * 2 + (z + dz) % 2 for dy, dz in relative]).astype(jnp.int32)


def tp_move(array, dy, dz):
    pairs = [(y * 2 + z, ((y + dy) % 4) * 2 + (z + dz) % 2) for y in range(4) for z in range(2)]
    return lax.ppermute(array, "tp", pairs)


def inst_move(array, dz, dx, dc):
    pairs = [
        (z * 8 + x * 2 + c, ((z + dz) % 2) * 8 + ((x + dx) % 4) * 2 + (c + dc) % 2)
        for z in range(2)
        for x in range(4)
        for c in range(2)
    ]
    return lax.ppermute(array, "inst", pairs)


def decode_kernel(
    rows, first_row, where, table, x0, x1, x2, x3, x4, x5, x6, x7, gain, wq, wk, wv, wo, pool,
    lane_row, query_gain, key_gain, plus, minus, local,
    x_v, wq_v, wk_v, wv_v, wo_v, pool_v, qkv, ctx, out_v, sems,
):
    steps = 4
    groups = 4
    width = x0.shape[2]
    count = steps * rows
    xs = (x0, x1, x2, x3, x4, x5, x6, x7)
    w_copies, o_copies = [], []
    for k in range(8):
        span = pl.ds(pl.multiple_of(where[k] * width, width), width)
        w_copies.append(
            (
                pltpu.make_async_copy(wq.at[span], wq_v.at[k], sems.at[0, k]),
                pltpu.make_async_copy(wk.at[span], wk_v.at[k], sems.at[1, k]),
                pltpu.make_async_copy(wv.at[span], wv_v.at[k], sems.at[2, k]),
            )
        )
        span = pl.ds(pl.multiple_of(where[8 + k] * width, 128), width)
        o_copies.append(pltpu.make_async_copy(wo.at[:, span], wo_v.at[k], sems.at[3, k]))
    pool_copy = pltpu.make_async_copy(pool, pool_v, sems.at[4, 0])
    x_copies = [
        pltpu.make_async_copy(xs[k].at[:, pl.ds(first_row, rows)], x_v.at[k], sems.at[5, k])
        for k in range(8)
    ]
    for copy in x_copies:
        copy.start()
    for trio in w_copies:
        for copy in trio:
            copy.start()
    pool_copy.start()
    for copy in o_copies:
        copy.start()

    square = jnp.zeros((count, 1), jnp.float32)
    for k in range(8):
        x_copies[k].wait()
        part = x_v[k].reshape(count, width).astype(jnp.float32)
        square = square + jnp.sum(part * part, axis=1, keepdims=True)
    inverse = lax.rsqrt(square * (1.0 / (8 * width)) + EPSILON)
    for k in range(8):
        for copy in w_copies[k]:
            copy.wait()
        normed = x_v[k].reshape(count, width).astype(jnp.float32) * inverse * gain[where[k]].astype(jnp.float32)
        normed = normed.astype(jnp.bfloat16)
        q_part = jnp.dot(normed, wq_v[k], preferred_element_type=jnp.float32)
        k_part = jnp.dot(normed, wk_v[k], preferred_element_type=jnp.float32)
        v_part = jnp.dot(normed, wv_v[k], preferred_element_type=jnp.float32)
        if k == 0:
            qkv[:, 0:512] = q_part
            qkv[:, 512:640] = k_part
            qkv[:, 640:768] = v_part
        else:
            qkv[:, 0:512] += q_part
            qkv[:, 512:640] += k_part
            qkv[:, 640:768] += v_part
    for head in range(5):
        lanes = slice(head * HEAD, (head + 1) * HEAD)
        raw = qkv[:, lanes]
        mean = jnp.mean(raw * raw, axis=1, keepdims=True)
        head_gain = (query_gain if head < 4 else key_gain)[...].astype(jnp.float32)
        qkv[:, lanes] = raw * lax.rsqrt(mean + EPSILON) * head_gain

    pool_copy.wait()
    height = steps * groups * GROUP
    query_row = lax.broadcasted_iota(jnp.int32, (height, 1), 0) % GROUP
    query_step = lax.broadcasted_iota(jnp.int32, (height, 1), 0) // (groups * GROUP)
    fresh_lane = lax.broadcasted_iota(jnp.int32, (1, steps * GROUP), 1)
    fresh_ok = (fresh_lane % GROUP == query_row) & (fresh_lane // GROUP <= query_step)
    scale = HEAD ** (-0.5)
    contract_last = (((1,), (1,)), ((), ()))

    def attend(i, carry):
        first = pl.multiple_of(i * GROUP, GROUP)

        def tiles(lane):
            return [
                qkv[pl.ds(pl.multiple_of(t * rows + first, GROUP), GROUP), lane * HEAD : (lane + 1) * HEAD]
                for t in range(steps)
            ]

        per_group = [tiles(g) for g in range(groups)]
        queries = jnp.concatenate(
            [per_group[g][t] for t in range(steps) for g in range(groups)], axis=0
        ).astype(jnp.bfloat16)
        fresh_k = jnp.concatenate(tiles(4), axis=0).astype(jnp.bfloat16)
        fresh_v = jnp.concatenate(tiles(5), axis=0).astype(jnp.bfloat16)
        blocks = [pool_v[table[first_row * 6 + i * (GROUP * 6) + j]] for j in range(GROUP * 6)]
        cached_k = jnp.concatenate([b[:, :HEAD] for b in blocks], axis=0)
        cached_v = jnp.concatenate([b[:, HEAD:] for b in blocks], axis=0)
        scores = lax.dot_general(queries, cached_k, contract_last, preferred_element_type=jnp.float32)
        fresh = lax.dot_general(queries, fresh_k, contract_last, preferred_element_type=jnp.float32)
        scores = jnp.where(lane_row[first_row // GROUP + i] == query_row, scores * scale, NEG)
        fresh = jnp.where(fresh_ok, fresh * scale, NEG)
        top = jnp.maximum(
            jnp.max(scores, axis=1, keepdims=True), jnp.max(fresh, axis=1, keepdims=True)
        )
        weights = jnp.exp(scores - top)
        fresh_weights = jnp.exp(fresh - top)
        total = jnp.sum(weights, axis=1, keepdims=True) + jnp.sum(
            fresh_weights, axis=1, keepdims=True
        )
        mixed = jnp.dot(weights.astype(jnp.bfloat16), cached_v, preferred_element_type=jnp.float32)
        mixed += jnp.dot(
            fresh_weights.astype(jnp.bfloat16), fresh_v, preferred_element_type=jnp.float32
        )
        mixed = mixed / total
        for t in range(steps):
            for g in range(groups):
                at = (t * groups + g) * GROUP
                ctx[
                    pl.ds(pl.multiple_of(t * rows + first, GROUP), GROUP),
                    g * HEAD : (g + 1) * HEAD,
                ] = mixed[at : at + GROUP]
        return carry

    lax.fori_loop(0, rows // GROUP, attend, 0, unroll=2)

    context = ctx[...].astype(jnp.bfloat16)
    outs = [plus.at[0], plus.at[1], minus.at[0], minus.at[1]] + [local.at[j] for j in range(4)]
    out_copies = []
    for k in range(8):
        o_copies[k].wait()
        out_v[k] = jnp.dot(context, wo_v[k], preferred_element_type=jnp.float32).astype(jnp.bfloat16)
        out_copies.append(pltpu.make_async_copy(out_v.at[k], outs[k], sems.at[6, k]))
        out_copies[k].start()
    for copy in out_copies:
        copy.wait()


def decode(
    rows, first_row, where, table, xs, gain, wq, wk, wv, wo, pool, lane_row, query_gain, key_gain
):
    steps, _, width = xs[0].shape
    count = steps * rows
    bf16, f32 = jnp.bfloat16, jnp.float32
    smem = pl.BlockSpec(memory_space=pltpu.SMEM)
    vmem = pl.BlockSpec(memory_space=pltpu.VMEM)
    hbm = pl.BlockSpec(memory_space=pltpu.HBM)
    return pl.pallas_call(
        functools.partial(decode_kernel, rows, first_row),
        out_shape=(
            jax.ShapeDtypeStruct((2, count, width), bf16),
            jax.ShapeDtypeStruct((2, count, width), bf16),
            jax.ShapeDtypeStruct((4, count, width), bf16),
        ),
        in_specs=[smem] * 2 + [hbm] * 8 + [vmem] + [hbm] * 5 + [vmem] * 3,
        out_specs=(hbm, hbm, hbm),
        scratch_shapes=[
            pltpu.VMEM((8, steps, rows, width), bf16),
            pltpu.VMEM((8, width, wq.shape[1]), bf16),
            pltpu.VMEM((8, width, wk.shape[1]), bf16),
            pltpu.VMEM((8, width, wv.shape[1]), bf16),
            pltpu.VMEM((8, wo.shape[0], width), bf16),
            pltpu.VMEM(pool.shape, bf16),
            pltpu.VMEM((count, 768), f32),
            pltpu.VMEM((count, 512), f32),
            pltpu.VMEM((8, count, width), bf16),
            pltpu.SemaphoreType.DMA((7, 8)),
        ],
        compiler_params=pltpu.CompilerParams(vmem_limit_bytes=60 * MIB),
        cost_estimate=pl.CostEstimate(
            flops=2 * count * 5120 * 1280, bytes_accessed=24 * MIB, transcendentals=0
        ),
        name="decode_rows",
    )(where, table, *xs, gain, wq, wk, wv, wo, pool, lane_row, query_gain, key_gain)


def slots_kernel(table, order, blocks, *refs):
    outs, (blocks_v, sems) = refs[:-7], refs[-2:]
    stages = refs[-7:-2]
    count = blocks.shape[0]
    load = pltpu.make_async_copy(blocks, blocks_v.at[pl.ds(0, count)], sems.at[0])
    load.start()
    blocks_v[count] = jnp.zeros(blocks.shape[1:], blocks.dtype)
    load.wait()
    copies = []
    if len(outs) == 5:

        def pick(m, carry):
            stages[4][m] = blocks_v[order[m]]
            return carry

        lax.fori_loop(0, outs[4].shape[0], pick, 0, unroll=16)
        copies.append(pltpu.make_async_copy(stages[4], outs[4], sems.at[5]))
        copies[0].start()
    for d in (2, 1, 3, 0):

        def one(j, carry):
            stages[d][j] = blocks_v[table[d * 2 * CAP + j]]
            return carry

        lax.fori_loop(0, 2 * CAP, one, 0, unroll=16)
        copies.append(pltpu.make_async_copy(stages[d], outs[d], sems.at[1 + d]))
        copies[-1].start()
    for copy in copies:
        copy.wait()


def fill_slots(table, order, blocks, with_compact):
    smem = pl.BlockSpec(memory_space=pltpu.SMEM)
    hbm = pl.BlockSpec(memory_space=pltpu.HBM)
    tail = blocks.shape[1:]
    heights = [2 * CAP] * 4 + [order.shape[0]] * with_compact
    return pl.pallas_call(
        slots_kernel,
        out_shape=tuple(jax.ShapeDtypeStruct((n,) + tail, blocks.dtype) for n in heights),
        in_specs=[smem, smem, hbm],
        out_specs=(hbm,) * len(heights),
        scratch_shapes=[pltpu.VMEM((2 * CAP,) + tail, blocks.dtype)] * 4
        + [
            pltpu.VMEM((order.shape[0],) + tail, blocks.dtype),
            pltpu.VMEM((blocks.shape[0] + 1,) + tail, blocks.dtype),
            pltpu.SemaphoreType.DMA((6,)),
        ],
        compiler_params=pltpu.CompilerParams(vmem_limit_bytes=60 * MIB),
        cost_estimate=pl.CostEstimate(flops=0, bytes_accessed=16 * MIB, transcendentals=0),
        name="fill_slots",
    )(table, order, blocks)


def slot_table(target, values, empty, own_z, own_x, own_c):
    order = jnp.arange(target.shape[0], dtype=jnp.int32)
    earlier = (target[:, None] == target[None, :]) & (order[None, :] < order[:, None])
    rank = jnp.sum(earlier.astype(jnp.int32), axis=1)
    slot = jnp.arange(8 * CAP, dtype=jnp.int32)
    far, other = slot // (2 * CAP), (slot // CAP) % 2
    wanted = own_z * 8 + ((own_x + far) % 4) * 2 + (own_c + other) % 2
    match = (wanted * CAP + slot % CAP)[:, None] == (target * CAP + rank)[None, :]
    return jnp.min(jnp.where(match, values[None, :], empty), axis=1)


def cross(received):
    return inst_move(jnp.concatenate([r[CAP:] for r in received]), 0, 0, 1)


def place_kernel(offsets, places_ref, *refs):
    count = len(offsets)
    arrays, out, stage, sems = refs[: max(offsets)[0] + 1], refs[-3], refs[-2], refs[-1]
    ins, outs = [], []
    for j, (which, offset) in enumerate(offsets):
        start = pl.multiple_of(places_ref[j] * CAP, CAP)
        part = arrays[which].at[pl.ds(offset * CAP, CAP)]
        ins.append(pltpu.make_async_copy(part, stage.at[j], sems.at[0, j]))
        outs.append(pltpu.make_async_copy(stage.at[j], out.at[pl.ds(start, CAP)], sems.at[1, j]))
    for copy in ins:
        copy.start()
    for j in range(count):
        ins[j].wait()
        outs[j].start()
    for copy in outs:
        copy.wait()


def place_pieces(where, arrays, offsets, before):
    smem = pl.BlockSpec(memory_space=pltpu.SMEM)
    either = pl.BlockSpec(memory_space=pl.ANY)
    hbm = pl.BlockSpec(memory_space=pltpu.HBM)
    blocks = arrays[0].shape[1:]
    shape = jax.ShapeDtypeStruct((16 * CAP,) + blocks, arrays[0].dtype)
    extra = [] if before is None else [before]
    return pl.pallas_call(
        functools.partial(place_kernel, tuple(offsets)),
        out_shape=shape,
        in_specs=[smem] + [either] * len(arrays) + [hbm] * len(extra),
        out_specs=hbm,
        scratch_shapes=[
            pltpu.VMEM((len(offsets), CAP) + blocks, arrays[0].dtype),
            pltpu.SemaphoreType.DMA((2, len(offsets))),
        ],
        input_output_aliases={} if before is None else {1 + len(arrays): 0},
        compiler_params=pltpu.CompilerParams(vmem_limit_bytes=60 * MIB),
        cost_estimate=pl.CostEstimate(flops=0, bytes_accessed=16 * MIB, transcendentals=0),
        name="place_pieces",
    )(where, *arrays, *extra)


def after(array, *others):
    return lax.optimization_barrier((array,) + others)[0]


def gather_rows(x, first):
    other = after(tp_move(x, 0, 1), *first)
    up, down = tp_move(x, 3, 0), tp_move(x, 1, 0)
    other_up, other_down = tp_move(other, 3, 0), tp_move(other, 1, 0)
    far = tp_move(down, 1, 0)
    other_far = tp_move(other_up, 3, 0)
    return [x, other, up, down, far, other_up, other_down, other_far]


def scatter_first(plus, minus, local):
    f32, bf16 = jnp.float32, jnp.bfloat16
    below = tp_move(plus, 1, 0)
    above = tp_move(minus, 3, 0)
    up = (local[0].astype(f32) + below[0].astype(f32)).astype(bf16)
    down = (local[1].astype(f32) + above[0].astype(f32)).astype(bf16)
    return below, above, up, down


def scatter_rest(local, below, above, up, down):
    f32, bf16 = jnp.float32, jnp.bfloat16
    from_below = tp_move(up, 1, 0)
    from_above = tp_move(down, 3, 0)
    other = (local[3].astype(f32) + below[1].astype(f32) + from_above.astype(f32)).astype(bf16)
    crossed = tp_move(other, 0, 1)
    mine = local[2].astype(f32) + above[1].astype(f32) + from_below.astype(f32)
    return (mine + crossed.astype(f32)).astype(bf16)


def body(
    inputs,
    norm_gain,
    query_weight,
    key_weight,
    value_weight,
    output_weight,
    query_gain,
    key_gain,
    kv_pool,
    block_table,
    cache_len,
    move_block,
    move_target,
):
    step_count, row_count, width = inputs.shape
    own = lax.axis_index("inst")
    own_z, own_x, own_c = own // 8, (own // 2) % 4, own % 2

    target = move_target[:, 0]
    other_target = inst_move(target, 1, 0, 0)

    table = slot_table(target, move_block, kv_pool.shape[0], own_z, own_x, own_c)
    *slots, compact = fill_slots(table, move_block, kv_pool, True)

    rows = row_count // CHUNKS
    gathered = gather_rows(inputs, (compact, other_target))
    compact = after(compact, *gathered[1:4])
    other_target = after(other_target, compact)
    other_blocks = inst_move(compact, 1, 0, 0)
    far = inst_move(slots[2], 0, 2, 0)
    near = inst_move(after(slots[1], far, *gathered), 0, 1, 0)
    back = inst_move(after(slots[3], far, *gathered), 0, 3, 0)
    order = jnp.arange(move_block.shape[0], dtype=jnp.int32)
    other_table = slot_table(other_target, order, order.shape[0], own_z, own_x, own_c)

    gain = norm_gain.reshape(8, 1, width)
    positions = jnp.arange(block_table.shape[1] * PAGE, dtype=jnp.int32)
    lane_row = jnp.where(
        positions[None, :] < cache_len[:, None],
        (jnp.arange(row_count, dtype=jnp.int32) % GROUP)[:, None],
        -1,
    ).reshape(row_count // GROUP, 1, -1)
    tp_where = places(GATHERED + SCATTERED)
    query_gain = query_gain.reshape(1, HEAD)
    key_gain = key_gain.reshape(1, HEAD)
    blocks_of_rows = block_table.reshape(-1)
    def where(z):
        return jnp.stack(
            [z * 8 + ((own_x - j % 4) % 4) * 2 + (own_c + j // 4) % 2 for j in range(8)]
        ).astype(jnp.int32)


    def decode_part(c):
        return decode(
            rows, c * rows, tp_where, blocks_of_rows, gathered, gain, query_weight, key_weight,
            value_weight, output_weight, kv_pool, lane_row, query_gain, key_gain,
        )

    plus, minus, local = decode_part(0)
    sums = scatter_first(plus, minus, local)
    other_table = after(other_table, near, back, plus)
    other_slots = fill_slots(other_table, order, other_blocks, False)
    other_far = inst_move(other_slots[2], 0, 2, 0)
    gathered[0] = after(gathered[0], other_slots[0])
    later_parts = decode_part(1)
    later_sums = scatter_first(*later_parts)
    chunks = [scatter_rest(local, *sums), scatter_rest(later_parts[2], *later_sums)]
    mixed_out = jnp.concatenate(
        [chunk.reshape(step_count, rows, width) for chunk in chunks], axis=1
    )

    def where(z, far_xs, cores):
        return jnp.stack(
            [z * 8 + ((own_x - dx) % 4) * 2 + (own_c + dc) % 2 for dc in cores for dx in far_xs]
        ).astype(jnp.int32)

    other_near = inst_move(after(other_slots[1], other_far, later_parts[0]), 0, 1, 0)
    other_back = inst_move(after(other_slots[3], other_far, later_parts[0]), 0, 3, 0)
    pieces = [slots[0], near, far, back]
    pieces.append(cross(after(pieces, later_parts[0])))
    offsets = [(j, 0) for j in range(4)] + [(4, j) for j in range(4)]
    arrived = place_pieces(where(own_z, (0, 1, 2, 3), (0, 1)), pieces, offsets, None)
    pieces = [other_slots[0], other_far]
    pieces.append(cross(after(pieces, later_parts[0])))
    offsets = [(0, 0), (1, 0), (2, 0), (2, 1)]
    arrived = place_pieces(where(1 - own_z, (0, 2), (0, 1)), pieces, offsets, arrived)
    pieces = [other_near, other_back]
    pieces.append(cross(pieces))
    arrived = place_pieces(where(1 - own_z, (1, 3), (0, 1)), pieces, offsets, arrived)
    return (mixed_out, arrived)


def solution(mesh):
    in_specs = (
        P(None, "inst", "tp"),
        P(),
        P(None, "tp"),
        P(None, "tp"),
        P(None, "tp"),
        P("tp", None),
        P(),
        P(),
        P("inst", None, "tp"),
        P("inst", None),
        P("inst"),
        P("inst"),
        P("inst", None),
    )
    out_specs = (P(None, "inst", "tp"), P("inst", None, "tp"))
    return jax.shard_map(body, mesh=mesh, in_specs=in_specs, out_specs=out_specs, check_vma=False)
```

```python
import functools

import jax
import jax.numpy as jnp
from jax import lax
from jax.experimental import pallas as pl
from jax.experimental.pallas import tpu as pltpu
from jax.sharding import PartitionSpec as P

HEAD = 128
CAP = 64
PAGE = 16
EPSILON = 1e-06
GROUP = 8
CHUNKS = 2
NEG = -1e30
MIB = 1024 * 1024

GATHERED = ((0, 0), (0, 1), (1, 0), (3, 0), (2, 0), (1, 1), (3, 1), (2, 1))
SCATTERED = ((2, 0), (1, 1), (2, 1), (3, 0), (1, 0), (3, 1), (0, 0), (0, 1))


def places(relative):
    me = lax.axis_index("tp")
    y, z = me // 2, me % 2
    return [((y + dy) % 4) * 2 + (z + dz) % 2 for dy, dz in relative]


def tp_move(array, dy, dz):
    pairs = [(y * 2 + z, ((y + dy) % 4) * 2 + (z + dz) % 2) for y in range(4) for z in range(2)]
    return lax.ppermute(array, "tp", pairs)


def inst_move(array, dz, dx, dc):
    pairs = [
        (z * 8 + x * 2 + c, ((z + dz) % 2) * 8 + ((x + dx) % 4) * 2 + (c + dc) % 2)
        for z in range(2)
        for x in range(4)
        for c in range(2)
    ]
    return lax.ppermute(array, "inst", pairs)


def decode_kernel(
    rows, first_row, table, lengths, x0, x1, x2, x3, x4, x5, x6, x7, gain, wq, wk, wv, wo, pool,
    query_gain, key_gain, plus, minus, local,
    x_v, wq_v, wk_v, wv_v, wo_v, pool_v, qkv, ctx, out_v, sems,
):
    steps = 4
    groups = 4
    width = x0.shape[2]
    count = steps * rows
    xs = (x0, x1, x2, x3, x4, x5, x6, x7)
    where = places(GATHERED + SCATTERED)
    w_copies, o_copies = [], []
    for k in range(8):
        span = pl.ds(pl.multiple_of(where[k] * width, width), width)
        w_copies.append(
            (
                pltpu.make_async_copy(wq.at[span], wq_v.at[k], sems.at[0, k]),
                pltpu.make_async_copy(wk.at[span], wk_v.at[k], sems.at[1, k]),
                pltpu.make_async_copy(wv.at[span], wv_v.at[k], sems.at[2, k]),
            )
        )
        span = pl.ds(pl.multiple_of(where[8 + k] * width, 128), width)
        o_copies.append(pltpu.make_async_copy(wo.at[:, span], wo_v.at[k], sems.at[3, k]))
    pool_copy = pltpu.make_async_copy(pool, pool_v, sems.at[4, 0])
    x_copies = [
        pltpu.make_async_copy(xs[k].at[:, pl.ds(first_row, rows)], x_v.at[k], sems.at[5, k])
        for k in range(8)
    ]
    for copy in x_copies:
        copy.start()
    for trio in w_copies:
        for copy in trio:
            copy.start()
    pool_copy.start()
    for copy in o_copies:
        copy.start()

    square = jnp.zeros((count, 1), jnp.float32)
    for k in range(8):
        x_copies[k].wait()
        part = x_v[k].reshape(count, width).astype(jnp.float32)
        square = square + jnp.sum(part * part, axis=1, keepdims=True)
    inverse = lax.rsqrt(square * (1.0 / (8 * width)) + EPSILON)
    for k in range(8):
        for copy in w_copies[k]:
            copy.wait()
        normed = x_v[k].reshape(count, width).astype(jnp.float32) * inverse * gain[where[k]].astype(jnp.float32)
        normed = normed.astype(jnp.bfloat16)
        q_part = jnp.dot(normed, wq_v[k], preferred_element_type=jnp.float32)
        k_part = jnp.dot(normed, wk_v[k], preferred_element_type=jnp.float32)
        v_part = jnp.dot(normed, wv_v[k], preferred_element_type=jnp.float32)
        if k == 0:
            qkv[:, 0:512] = q_part
            qkv[:, 512:640] = k_part
            qkv[:, 640:768] = v_part
        else:
            qkv[:, 0:512] += q_part
            qkv[:, 512:640] += k_part
            qkv[:, 640:768] += v_part
    for head in range(5):
        lanes = slice(head * HEAD, (head + 1) * HEAD)
        raw = qkv[:, lanes]
        mean = jnp.mean(raw * raw, axis=1, keepdims=True)
        head_gain = (query_gain if head < 4 else key_gain)[...].astype(jnp.float32)
        qkv[:, lanes] = raw * lax.rsqrt(mean + EPSILON) * head_gain

    pool_copy.wait()
    height = steps * groups * GROUP
    query_row = lax.broadcasted_iota(jnp.int32, (height, 1), 0) % GROUP
    query_step = lax.broadcasted_iota(jnp.int32, (height, 1), 0) // (groups * GROUP)
    fresh_lane = lax.broadcasted_iota(jnp.int32, (1, steps * GROUP), 1)
    fresh_ok = (fresh_lane % GROUP == query_row) & (fresh_lane // GROUP <= query_step)
    lane = lax.broadcasted_iota(jnp.int32, (1, GROUP * 6 * PAGE), 1)
    lane_row, lane_place = lane // (6 * PAGE), lane % (6 * PAGE)
    scale = HEAD ** (-0.5)
    contract_last = (((1,), (1,)), ((), ()))

    def attend(i, carry):
        first = pl.multiple_of(i * GROUP, GROUP)

        def tiles(lane):
            return [
                qkv[pl.ds(pl.multiple_of(t * rows + first, GROUP), GROUP), lane * HEAD : (lane + 1) * HEAD]
                for t in range(steps)
            ]

        per_group = [tiles(g) for g in range(groups)]
        queries = jnp.concatenate(
            [per_group[g][t] for t in range(steps) for g in range(groups)], axis=0
        ).astype(jnp.bfloat16)
        fresh_k = jnp.concatenate(tiles(4), axis=0).astype(jnp.bfloat16)
        fresh_v = jnp.concatenate(tiles(5), axis=0).astype(jnp.bfloat16)
        blocks = [pool_v[table[j % 6, first_row + i * GROUP + j // 6]] for j in range(GROUP * 6)]
        cached_k = jnp.concatenate([b[:, :HEAD] for b in blocks], axis=0)
        cached_v = jnp.concatenate([b[:, HEAD:] for b in blocks], axis=0)
        scores = lax.dot_general(queries, cached_k, contract_last, preferred_element_type=jnp.float32)
        fresh = lax.dot_general(queries, fresh_k, contract_last, preferred_element_type=jnp.float32)
        used = jnp.full(lane.shape, -1, jnp.int32)
        for r in range(GROUP):
            length = lengths[first_row + i * GROUP + r]
            used = jnp.where((lane_row == r) & (lane_place < length), r, used)
        scores = jnp.where(used == query_row, scores * scale, NEG)
        fresh = jnp.where(fresh_ok, fresh * scale, NEG)
        top = jnp.maximum(
            jnp.max(scores, axis=1, keepdims=True), jnp.max(fresh, axis=1, keepdims=True)
        )
        weights = jnp.exp(scores - top)
        fresh_weights = jnp.exp(fresh - top)
        total = jnp.sum(weights, axis=1, keepdims=True) + jnp.sum(
            fresh_weights, axis=1, keepdims=True
        )
        mixed = jnp.dot(weights.astype(jnp.bfloat16), cached_v, preferred_element_type=jnp.float32)
        mixed += jnp.dot(
            fresh_weights.astype(jnp.bfloat16), fresh_v, preferred_element_type=jnp.float32
        )
        mixed = mixed / total
        for t in range(steps):
            for g in range(groups):
                at = (t * groups + g) * GROUP
                ctx[
                    pl.ds(pl.multiple_of(t * rows + first, GROUP), GROUP),
                    g * HEAD : (g + 1) * HEAD,
                ] = mixed[at : at + GROUP]
        return carry

    lax.fori_loop(0, rows // GROUP, attend, 0, unroll=2)

    context = ctx[...].astype(jnp.bfloat16)
    outs = [plus.at[0], plus.at[1], minus.at[0], minus.at[1]] + [local.at[j] for j in range(4)]
    out_copies = []
    for k in range(8):
        o_copies[k].wait()
        out_v[k] = jnp.dot(context, wo_v[k], preferred_element_type=jnp.float32).astype(jnp.bfloat16)
        out_copies.append(pltpu.make_async_copy(out_v.at[k], outs[k], sems.at[6, k]))
        out_copies[k].start()
    for copy in out_copies:
        copy.wait()


def decode(
    rows, first_row, table, lengths, xs, gain, wq, wk, wv, wo, pool, query_gain, key_gain
):
    steps, _, width = xs[0].shape
    count = steps * rows
    bf16, f32 = jnp.bfloat16, jnp.float32
    smem = pl.BlockSpec(memory_space=pltpu.SMEM)
    vmem = pl.BlockSpec(memory_space=pltpu.VMEM)
    hbm = pl.BlockSpec(memory_space=pltpu.HBM)
    return pl.pallas_call(
        functools.partial(decode_kernel, rows, first_row),
        out_shape=(
            jax.ShapeDtypeStruct((2, count, width), bf16),
            jax.ShapeDtypeStruct((2, count, width), bf16),
            jax.ShapeDtypeStruct((4, count, width), bf16),
        ),
        in_specs=[smem] * 2 + [hbm] * 8 + [vmem] + [hbm] * 5 + [vmem] * 2,
        out_specs=(hbm, hbm, hbm),
        scratch_shapes=[
            pltpu.VMEM((8, steps, rows, width), bf16),
            pltpu.VMEM((8, width, wq.shape[1]), bf16),
            pltpu.VMEM((8, width, wk.shape[1]), bf16),
            pltpu.VMEM((8, width, wv.shape[1]), bf16),
            pltpu.VMEM((8, wo.shape[0], width), bf16),
            pltpu.VMEM(pool.shape, bf16),
            pltpu.VMEM((count, 768), f32),
            pltpu.VMEM((count, 512), f32),
            pltpu.VMEM((8, count, width), bf16),
            pltpu.SemaphoreType.DMA((7, 8)),
        ],
        compiler_params=pltpu.CompilerParams(vmem_limit_bytes=60 * MIB),
        cost_estimate=pl.CostEstimate(
            flops=2 * count * 5120 * 1280, bytes_accessed=24 * MIB, transcendentals=0
        ),
        name="decode_rows",
    )(table, lengths, *xs, gain, wq, wk, wv, wo, pool, query_gain, key_gain)


def slots_kernel(table, order, blocks, *refs):
    outs, (blocks_v, sems) = refs[:-7], refs[-2:]
    stages = refs[-7:-2]
    count = blocks.shape[0]
    load = pltpu.make_async_copy(blocks, blocks_v.at[pl.ds(0, count)], sems.at[0])
    load.start()
    blocks_v[count] = jnp.zeros(blocks.shape[1:], blocks.dtype)
    load.wait()
    copies = []
    if len(outs) == 5:

        def pick(m, carry):
            stages[4][m] = blocks_v[order[m]]
            return carry

        lax.fori_loop(0, outs[4].shape[0], pick, 0, unroll=16)
        copies.append(pltpu.make_async_copy(stages[4], outs[4], sems.at[5]))
        copies[0].start()
    for d in (2, 1, 3, 0):

        def one(j, carry):
            stages[d][j] = blocks_v[table[d * 2 * CAP + j]]
            return carry

        lax.fori_loop(0, 2 * CAP, one, 0, unroll=16)
        copies.append(pltpu.make_async_copy(stages[d], outs[d], sems.at[1 + d]))
        copies[-1].start()
    for copy in copies:
        copy.wait()


def fill_slots(table, order, blocks, with_compact):
    smem = pl.BlockSpec(memory_space=pltpu.SMEM)
    hbm = pl.BlockSpec(memory_space=pltpu.HBM)
    tail = blocks.shape[1:]
    heights = [2 * CAP] * 4 + [order.shape[0]] * with_compact
    return pl.pallas_call(
        slots_kernel,
        out_shape=tuple(jax.ShapeDtypeStruct((n,) + tail, blocks.dtype) for n in heights),
        in_specs=[smem, smem, hbm],
        out_specs=(hbm,) * len(heights),
        scratch_shapes=[pltpu.VMEM((2 * CAP,) + tail, blocks.dtype)] * 4
        + [
            pltpu.VMEM((order.shape[0] if with_compact else 8,) + tail, blocks.dtype),
            pltpu.VMEM((blocks.shape[0] + 1,) + tail, blocks.dtype),
            pltpu.SemaphoreType.DMA((6,)),
        ],
        compiler_params=pltpu.CompilerParams(vmem_limit_bytes=60 * MIB),
        cost_estimate=pl.CostEstimate(flops=0, bytes_accessed=16 * MIB, transcendentals=0),
        name="fill_slots",
    )(table, order, blocks)


def slot_table(target, values, empty, own_z, own_x, own_c):
    order = jnp.arange(target.shape[0], dtype=jnp.int32)
    earlier = (target[:, None] == target[None, :]) & (order[None, :] < order[:, None])
    rank = jnp.sum(earlier.astype(jnp.int32), axis=1)
    slot = jnp.arange(8 * CAP, dtype=jnp.int32)
    far, other = slot // (2 * CAP), (slot // CAP) % 2
    wanted = own_z * 8 + ((own_x + far) % 4) * 2 + (own_c + other) % 2
    match = (wanted * CAP + slot % CAP)[:, None] == (target * CAP + rank)[None, :]
    return jnp.min(jnp.where(match, values[None, :], empty), axis=1)


def cross(received):
    offsets = [(j, 1) for j in range(len(received))]
    order = jnp.arange(len(received), dtype=jnp.int32)
    return inst_move(place_pieces(order, received, offsets, None, len(received)), 0, 0, 1)


def place_kernel(offsets, places_ref, *refs):
    count = len(offsets)
    arrays, out, stage, sems = refs[: max(offsets)[0] + 1], refs[-3], refs[-2], refs[-1]
    ins, outs = [], []
    for j, (which, offset) in enumerate(offsets):
        start = pl.multiple_of(places_ref[j] * CAP, CAP)
        part = arrays[which].at[pl.ds(offset * CAP, CAP)]
        ins.append(pltpu.make_async_copy(part, stage.at[j], sems.at[0, j]))
        outs.append(pltpu.make_async_copy(stage.at[j], out.at[pl.ds(start, CAP)], sems.at[1, j]))
    for copy in ins:
        copy.start()
    for j in range(count):
        ins[j].wait()
        outs[j].start()
    for copy in outs:
        copy.wait()


def place_pieces(where, arrays, offsets, before, count=16):
    smem = pl.BlockSpec(memory_space=pltpu.SMEM)
    either = pl.BlockSpec(memory_space=pl.ANY)
    hbm = pl.BlockSpec(memory_space=pltpu.HBM)
    blocks = arrays[0].shape[1:]
    shape = jax.ShapeDtypeStruct((count * CAP,) + blocks, arrays[0].dtype)
    extra = [] if before is None else [before]
    return pl.pallas_call(
        functools.partial(place_kernel, tuple(offsets)),
        out_shape=shape,
        in_specs=[smem] + [either] * len(arrays) + [hbm] * len(extra),
        out_specs=hbm,
        scratch_shapes=[
            pltpu.VMEM((len(offsets), CAP) + blocks, arrays[0].dtype),
            pltpu.SemaphoreType.DMA((2, len(offsets))),
        ],
        input_output_aliases={} if before is None else {1 + len(arrays): 0},
        compiler_params=pltpu.CompilerParams(vmem_limit_bytes=60 * MIB),
        cost_estimate=pl.CostEstimate(flops=0, bytes_accessed=16 * MIB, transcendentals=0),
        name="place_pieces",
    )(where, *arrays, *extra)


def after(array, *others):
    return lax.optimization_barrier((array,) + others)[0]


def gather_rows(x, first):
    other = after(tp_move(x, 0, 1), *first)
    up, down = tp_move(x, 3, 0), tp_move(x, 1, 0)
    other_up, other_down = tp_move(other, 3, 0), tp_move(other, 1, 0)
    far = tp_move(down, 1, 0)
    other_far = tp_move(other_up, 3, 0)
    return [x, other, up, down, far, other_up, other_down, other_far]


def scatter_first(plus, minus, local):
    f32, bf16 = jnp.float32, jnp.bfloat16
    below = tp_move(plus, 1, 0)
    above = tp_move(minus, 3, 0)
    up = (local[0].astype(f32) + below[0].astype(f32)).astype(bf16)
    down = (local[1].astype(f32) + above[0].astype(f32)).astype(bf16)
    return below, above, up, down


def scatter_second(up, down):
    return tp_move(up, 1, 0), tp_move(down, 3, 0)


def scatter_third(local, below, from_above):
    f32 = jnp.float32
    total = local[3].astype(f32) + below[1].astype(f32) + from_above.astype(f32)
    return total.astype(jnp.bfloat16)


def scatter_last(local, above, from_below, crossed):
    f32 = jnp.float32
    mine = local[2].astype(f32) + above[1].astype(f32) + from_below.astype(f32)
    return (mine + crossed.astype(f32)).astype(jnp.bfloat16)


def body(
    inputs,
    norm_gain,
    query_weight,
    key_weight,
    value_weight,
    output_weight,
    query_gain,
    key_gain,
    kv_pool,
    block_table,
    cache_len,
    move_block,
    move_target,
):
    step_count, row_count, width = inputs.shape
    own = lax.axis_index("inst")
    own_z, own_x, own_c = own // 8, (own // 2) % 4, own % 2

    target = move_target[:, 0]
    other_target = inst_move(target, 1, 0, 0)

    table = slot_table(target, move_block, kv_pool.shape[0], own_z, own_x, own_c)
    *slots, compact = fill_slots(table, move_block, kv_pool, True)

    rows = row_count // CHUNKS
    gathered = gather_rows(inputs, (compact, other_target))
    compact = after(compact, *gathered[1:4])
    other_target = after(other_target, compact)
    other_blocks = inst_move(compact, 1, 0, 0)
    far = inst_move(slots[2], 0, 2, 0)
    near = inst_move(after(slots[1], far, *gathered), 0, 1, 0)
    back = inst_move(after(slots[3], far, *gathered), 0, 3, 0)
    order = jnp.arange(move_block.shape[0], dtype=jnp.int32)
    other_table = slot_table(other_target, order, order.shape[0], own_z, own_x, own_c)

    gain = norm_gain.reshape(8, 1, width)
    query_gain = query_gain.reshape(1, HEAD)
    key_gain = key_gain.reshape(1, HEAD)
    blocks_of_rows = block_table.T
    def where(z):
        return jnp.stack(
            [z * 8 + ((own_x - j % 4) % 4) * 2 + (own_c + j // 4) % 2 for j in range(8)]
        ).astype(jnp.int32)


    def decode_part(c):
        return decode(
            rows, c * rows, blocks_of_rows, cache_len, gathered, gain, query_weight, key_weight,
            value_weight, output_weight, kv_pool, query_gain, key_gain,
        )

    plus, minus, local = decode_part(0)
    sums = scatter_first(plus, minus, local)
    other_table = after(other_table, near, back, plus)
    other_slots = fill_slots(other_table, other_table, other_blocks, False)
    other_far = inst_move(other_slots[2], 0, 2, 0)
    gathered[0] = after(gathered[0], other_slots[0], *sums[2:])
    seconds = scatter_second(*sums[2:])
    later_parts = decode_part(1)
    later_sums = scatter_first(
        after(later_parts[0], *seconds), after(later_parts[1], *seconds), later_parts[2]
    )
    later_seconds = scatter_second(*later_sums[2:])
    other_near = inst_move(after(other_slots[1], other_far, later_parts[0]), 0, 1, 0)
    other_back = inst_move(after(other_slots[3], other_far, later_parts[0]), 0, 3, 0)

    def where(z):
        return jnp.stack(
            [z * 8 + ((own_x - dx) % 4) * 2 + (own_c + dc) % 2 for dc in (0, 1) for dx in range(4)]
        ).astype(jnp.int32)

    offsets = [(j, 0) for j in range(4)] + [(4, j) for j in range(4)]
    pieces = [slots[0], near, far, back]
    pieces.append(cross(after(pieces, *seconds)))
    arrived = place_pieces(where(own_z), pieces, offsets, None)
    other = scatter_third(local, sums[0], seconds[1])
    chunks = [scatter_last(local, sums[1], seconds[0], tp_move(other, 0, 1))]
    later = scatter_third(later_parts[2], later_sums[0], after(later_seconds[1], later_seconds[0]))
    later_crossed = after(tp_move(later, 0, 1), arrived)
    chunks.append(scatter_last(later_parts[2], later_sums[1], later_seconds[0], later_crossed))
    mixed_out = jnp.concatenate(
        [chunk.reshape(step_count, rows, width) for chunk in chunks], axis=1
    )
    pieces = [other_slots[0], other_near, other_far, other_back]
    pieces.append(cross(after(pieces, later, chunks[0])))
    pieces[0] = after(pieces[0], mixed_out)
    arrived = place_pieces(where(1 - own_z), pieces, offsets, arrived)
    return (mixed_out, arrived)


def solution(mesh):
    in_specs = (
        P(None, "inst", "tp"),
        P(),
        P(None, "tp"),
        P(None, "tp"),
        P(None, "tp"),
        P("tp", None),
        P(),
        P(),
        P("inst", None, "tp"),
        P("inst", None),
        P("inst"),
        P("inst"),
        P("inst", None),
    )
    out_specs = (P(None, "inst", "tp"), P("inst", None, "tp"))
    return jax.shard_map(body, mesh=mesh, in_specs=in_specs, out_specs=out_specs, check_vma=False)
```
